32 devices in a mesh: groups: 2 (over y), tensor: 4 (over z), dp: 4 (over x, core).
Axes of the slice: x: 2, y: 2, z: 4, core: 2. Of those that a mesh axis runs over, the one named last changes fastest.
Arguments:
- hidden: bfloat16 [4096, 8192], P(('groups', 'dp'), 'tensor'), parts along dimension 0, may hold values from -6 to 6
- output_weight: bfloat16 [8192, 8192], P('tensor'), may hold values from -0.0625 to 0.0625
- adapter_down_maps: bfloat16 [256, 64, 8192], P('dp', None, 'tensor'), may hold values from -0.0625 to 0.0625
- adapter_up_maps: bfloat16 [256, 64, 8192], P('dp', None, 'tensor'), may hold values from -0.75 to 0.75
- adapter_slot: int32 [512], P('groups'), parts along dimension 0, may hold values from 0 to 255, as said below
- segment_adapter: int32 [256], P(('groups', 'dp')), parts along dimension 0, may hold values from 0 to 255, as said below
Outputs:
- projected: bfloat16 [4096, 8192], P(('groups', 'dp'), 'tensor'), parts along dimension 0
The draws below stay inside these ranges and needn't reach their ends.
There are 2 independent parts, one for each index of `groups`. The reference program is written for one: setup_inputs(seed, part) draws one part's arguments, and reference() takes and returns one part's arrays. A program takes and returns all parts, laid end to end along the dimension named above; an argument that names none is the same for every part. Nothing has to cross between parts.
Inputs may be any that keep to these rules, and one draw needn't show every extreme that they name: adapter_slot names each of the 256 slots once; slot q is stored on dp index q // 64. `segment_adapter`: among the 32 blocks of one dp index, at most 16 have adapters stored on any one dp index; in every draw one dp index holds the adapters of exactly 16 blocks of every dp index.
All inputs are finite; a program needn't handle non-finite values.
Results may differ from the reference program's by a relative error of at most 0.001.
Values may be sent and summed in bfloat16 or wider, within the bound.
A program may use at most 256 MiB of HBM per device.

```python
import jax
import jax.numpy as jnp
from jax import lax

MODEL_WIDTH = 8192
ADAPTER_RANK = 64
BLK = 16
SEG_DEV = 32
SLOT_DEV = 64
SEGMENTS = 128
REQUEST_TOTAL = 2048
ADAPTER_TOTAL = 256


def slot_table(key):
    return jax.random.permutation(jax.random.fold_in(key, 11), ADAPTER_TOTAL).astype(jnp.int32)


def draw_adapter_slot(key, part):
    return slot_table(key)


def draw_segment_adapter(key, part):
    slot_perm = slot_table(key)
    key = jax.random.fold_in(key, 5)
    key_hot, key_mix, key_top, key_low = jax.random.split(key, 4)
    home_count = ADAPTER_TOTAL // SLOT_DEV
    device_count = SEGMENTS // SEG_DEV
    half_count = SEG_DEV // 2
    hot_home = jax.random.randint(key_hot, (), 0, home_count)
    order = jnp.arange(SEG_DEV, dtype=jnp.int32)
    others = (hot_home + 1 + (order - half_count) % (home_count - 1)) % home_count
    base_home = jnp.where(order < half_count, hot_home, others)
    mix_keys = jax.random.split(key_mix, device_count)
    shuffles = jax.vmap(lambda k: jax.random.permutation(k, SEG_DEV))(mix_keys)
    homes = base_home[shuffles]
    upper = jax.random.randint(key_top, (device_count, SEG_DEV), 0, SLOT_DEV)
    within = jax.random.randint(key_low, (device_count, SEG_DEV), 0, upper + 1)
    slots = homes * SLOT_DEV + within
    inverse = jnp.argsort(slot_perm).astype(jnp.int32)
    return inverse[slots].reshape(SEGMENTS).astype(jnp.int32)


def level_of(own_key, dims, pieces, smallest, top_value):
    loudness = 1.0
    for dim, blocks in pieces:
        draws = jax.random.uniform(jax.random.fold_in(jax.random.fold_in(own_key, 6), dim), (blocks,), jnp.float32, smallest / len(pieces), top_value / len(pieces))
        loudness = loudness * jnp.repeat(jnp.exp(draws), dims[dim] // blocks).reshape((-1,) + (1,) * (len(dims) - 1 - dim))
    return loudness


def noise(rng, extent, scale, bound, pieces=(), held_as=jnp.bfloat16):
    values = jax.random.normal(rng, extent, jnp.float32) * scale
    if len(pieces) > 0:
        values = level_of(rng, extent, pieces, -0.22, 0.18) * values
    return jnp.clip(values, min=-bound, max=bound).astype(held_as)


def setup_inputs(seed: int = 0, part: int = 0) -> dict:
    key_of = jax.random.split(jax.random.key(seed), 7)
    part_splits = jax.random.split(jax.random.fold_in(key_of[6], part), 7)
    return {
        "hidden": noise(part_splits[0], (REQUEST_TOTAL, MODEL_WIDTH), 1.0, 6.0, ((0, 4), (1, 4))),
        "output_weight": noise(key_of[1], (MODEL_WIDTH, MODEL_WIDTH), MODEL_WIDTH ** -0.5, 0.0625, ((0, 4),)),
        "adapter_down_maps": noise(key_of[2], (ADAPTER_TOTAL, ADAPTER_RANK, MODEL_WIDTH), MODEL_WIDTH ** -0.5, 0.0625, ((0, 4), (2, 4))),
        "adapter_up_maps": noise(key_of[3], (ADAPTER_TOTAL, ADAPTER_RANK, MODEL_WIDTH), ADAPTER_RANK ** -0.5, 0.75, ((0, 4), (2, 4))),
        "adapter_slot": draw_adapter_slot(jax.random.fold_in(jax.random.fold_in(key_of[6], part), 71), part),
        "segment_adapter": draw_segment_adapter(jax.random.fold_in(jax.random.fold_in(key_of[6], part), 71), part),
    }


def reference(hidden, output_weight, adapter_down_maps, adapter_up_maps, adapter_slot, segment_adapter):
    base_projection_sum = jnp.dot(hidden, output_weight, preferred_element_type=jnp.float32)
    storage_slot_index = adapter_slot[segment_adapter].astype(jnp.int32)
    segment_rows = hidden.reshape(SEGMENTS, BLK, MODEL_WIDTH)

    def segment_update(operands):
        block_rows, slot_position = operands
        down_matrix_block = lax.dynamic_index_in_dim(adapter_down_maps, slot_position, 0, keepdims=False)
        up_matrix_block = lax.dynamic_index_in_dim(adapter_up_maps, slot_position, 0, keepdims=False)
        rank_sum = jnp.dot(block_rows, down_matrix_block.T, preferred_element_type=jnp.float32)
        return jnp.dot(rank_sum, up_matrix_block.astype(jnp.float32), precision=lax.Precision.HIGHEST)

    adapter_delta = lax.map(segment_update, (segment_rows, storage_slot_index))
    return (base_projection_sum + adapter_delta.reshape(REQUEST_TOTAL, MODEL_WIDTH)).astype(jnp.bfloat16)
```

```python
import functools

import jax
import jax.numpy as jnp
from jax import lax
from jax.experimental import pallas as pl
from jax.experimental.pallas import tpu as pltpu
from jax.sharding import PartitionSpec as P

MIB = 1024 * 1024
STEP = 8


def down_kernel(step, slots_ref, rows_ref, *refs):
    maps, out_ref = refs[:step], refs[step]
    for i in range(step):
        out_ref[i] = lax.dot_general(
            rows_ref[i], maps[i][0], (((1,), (1,)), ((), ())),
            preferred_element_type=jnp.float32,
        )


def up_kernel(step, slots_ref, rank_ref, *refs):
    maps, out_ref = refs[:step], refs[step]
    for i in range(step):
        rank = rank_ref[i]
        block = rank.shape[0]
        high = rank.astype(jnp.bfloat16)
        rest = rank - high.astype(jnp.float32)
        mid = rest.astype(jnp.bfloat16)
        low = (rest - mid.astype(jnp.float32)).astype(jnp.bfloat16)
        parts = jnp.concatenate([high, mid, low], axis=0)
        got = jnp.dot(parts, maps[i][0], preferred_element_type=jnp.float32)
        out_ref[i] = (got[2 * block:] + got[block:2 * block]) + got[:block]


def map_specs(step, maps):
    shape = (1,) + maps.shape[1:]

    def spec(i):
        return pl.BlockSpec(shape, lambda g, slots: (slots[g * step + i], 0, 0))

    return [spec(i) for i in range(step)]


def apply_maps(kernel, slots, values, maps, out_tail):
    count = slots.shape[0]
    step = STEP if count % STEP == 0 else 1
    tail = values.shape[1:]
    return pl.pallas_call(
        functools.partial(kernel, step),
        grid_spec=pltpu.PrefetchScalarGridSpec(
            num_scalar_prefetch=1,
            grid=(count // step,),
            in_specs=[pl.BlockSpec((step,) + tail, lambda g, slots: (g, 0, 0))]
            + map_specs(step, maps),
            out_specs=pl.BlockSpec((step,) + out_tail, lambda g, slots: (g, 0, 0)),
        ),
        out_shape=jax.ShapeDtypeStruct((count,) + out_tail, jnp.float32),
        compiler_params=pltpu.CompilerParams(vmem_limit_bytes=40 * MIB),
    )(slots, values, *([maps] * step))


def shift(x, by, count):
    return lax.ppermute(x, "dp", [(i, (i + by) % count) for i in range(count)])


def per_device(
    hidden, output_weight, adapter_down_maps, adapter_up_maps, adapter_slot, segment_adapter
):
    rows, width = hidden.shape
    segs = segment_adapter.shape[0]
    block = rows // segs
    stored, rank_dim, _ = adapter_down_maps.shape
    dp = lax.axis_size("dp")
    me = lax.axis_index("dp")
    cap = segs // 2
    slot = adapter_slot[segment_adapter]
    rel = (slot // stored - me) % dp
    local = slot % stored
    mask = rel[None, :] == jnp.arange(dp, dtype=jnp.int32)[:, None]
    running = jnp.cumsum(mask.astype(jnp.int32), axis=1) - 1
    position = jnp.sum(jnp.where(mask, running, 0), axis=0)
    match = mask[:, None, :] & (
        position[None, None, :] == jnp.arange(cap, dtype=jnp.int32)[None, :, None]
    )
    picked = jnp.sum(
        jnp.where(match, jnp.arange(segs, dtype=jnp.int32)[None, None, :], 0), axis=2
    )
    wanted = jnp.sum(jnp.where(match, local[None, None, :], 0), axis=2)
    place = rel * cap + position
    seg_rows = hidden.reshape(segs, block, width)
    out_rows = seg_rows[picked]
    got_slots = [wanted[0]] + [shift(wanted[k], k, dp) for k in range(1, dp)]
    got_rows = [out_rows[0]] + [shift(out_rows[k], k, dp) for k in range(1, dp)]
    slots = jnp.concatenate(got_slots)
    there_rows = jnp.concatenate(got_rows)
    rank = apply_maps(down_kernel, slots, there_rows, adapter_down_maps, (block, rank_dim))
    rank = lax.psum(rank, "tensor")
    delta = apply_maps(up_kernel, slots, rank, adapter_up_maps, (block, width))
    delta = delta.reshape(dp, cap, block, width)
    back = [delta[0]] + [shift(delta[k], dp - k, dp) for k in range(1, dp)]
    delta_rows = jnp.concatenate(back)[place].reshape(rows, width)
    base = lax.psum_scatter(
        lax.dot_general(
            output_weight, hidden, (((0,), (1,)), ((), ())), preferred_element_type=jnp.float32
        ),
        "tensor",
        scatter_dimension=0,
        tiled=True,
    ).T
    return (base + delta_rows).astype(jnp.bfloat16)


def solution(mesh):
    return jax.shard_map(
        per_device,
        mesh=mesh,
        in_specs=(
            P(("groups", "dp"), "tensor"),
            P("tensor", None),
            P("dp", None, "tensor"),
            P("dp", None, "tensor"),
            P("groups"),
            P(("groups", "dp")),
        ),
        out_specs=P(("groups", "dp"), "tensor"),
        check_vma=False,
    )
```

```python
import functools

import jax
import jax.numpy as jnp
from jax import lax
from jax.experimental import pallas as pl
from jax.experimental.pallas import tpu as pltpu
from jax.sharding import PartitionSpec as P

MIB = 1024 * 1024
STEP = 8


def down_kernel(step, slots_ref, rows_ref, *refs):
    maps, out_ref = refs[:step], refs[step]
    for i in range(step):
        out_ref[i] = lax.dot_general(
            rows_ref[i], maps[i][0], (((1,), (1,)), ((), ())),
            preferred_element_type=jnp.float32,
        )


def up_kernel(step, slots_ref, rank_ref, *refs):
    maps, out_ref = refs[:step], refs[step]
    for i in range(step):
        rank = rank_ref[i]
        block = rank.shape[0]
        high = rank.astype(jnp.bfloat16)
        rest = rank - high.astype(jnp.float32)
        mid = rest.astype(jnp.bfloat16)
        low = (rest - mid.astype(jnp.float32)).astype(jnp.bfloat16)
        parts = jnp.concatenate([high, mid, low], axis=0)
        got = jnp.dot(parts, maps[i][0], preferred_element_type=jnp.float32)
        out_ref[i] = (got[2 * block:] + got[block:2 * block]) + got[:block]


def map_specs(step, maps):
    shape = (1,) + maps.shape[1:]

    def spec(i):
        return pl.BlockSpec(shape, lambda g, slots: (slots[g * step + i], 0, 0))

    return [spec(i) for i in range(step)]


def apply_maps(kernel, slots, values, maps, out_tail):
    count = slots.shape[0]
    step = STEP if count % STEP == 0 else 1
    tail = values.shape[1:]
    return pl.pallas_call(
        functools.partial(kernel, step),
        grid_spec=pltpu.PrefetchScalarGridSpec(
            num_scalar_prefetch=1,
            grid=(count // step,),
            in_specs=[pl.BlockSpec((step,) + tail, lambda g, slots: (g, 0, 0))]
            + map_specs(step, maps),
            out_specs=pl.BlockSpec((step,) + out_tail, lambda g, slots: (g, 0, 0)),
        ),
        out_shape=jax.ShapeDtypeStruct((count,) + out_tail, jnp.float32),
        compiler_params=pltpu.CompilerParams(vmem_limit_bytes=40 * MIB),
    )(slots, values, *([maps] * step))


FINE = 128.0
TOP = 32767.0
MESH = pl.DeviceIdType.MESH


def pack(ref, at, value):
    rows, cols = value.shape
    top = jnp.maximum(jnp.max(jnp.abs(value), axis=0, keepdims=True), 1e-30)
    code = jnp.ceil(jnp.log2(top) * FINE + 0.125)
    scale = jnp.exp2(code * (1.0 / FINE))
    whole = jnp.round(jnp.clip(value * (TOP / scale), -TOP, TOP))
    ref[at, :rows, :] = whole.astype(jnp.int32).astype(jnp.int16)
    ref[at, rows:, :] = jnp.broadcast_to(code.astype(jnp.int32), (16, cols)).astype(jnp.int16)


def unpack(ref, at, rows):
    code = ref[at, rows:, :].astype(jnp.int32).astype(jnp.float32)[:1]
    scale = jnp.exp2(code * (1.0 / FINE)) * (1.0 / TOP)
    return ref[at, :rows, :].astype(jnp.int32).astype(jnp.float32) * scale


def greet(axis, me, last):
    barrier = pltpu.get_barrier_semaphore()

    @pl.when(me > 0)
    def _():
        pl.semaphore_signal(barrier, inc=1, device_id={axis: me - 1}, device_id_type=MESH)

    @pl.when(me < last)
    def _():
        pl.semaphore_signal(barrier, inc=1, device_id={axis: me + 1}, device_id_type=MESH)

    ends = jnp.logical_or(me == 0, me == last)

    @pl.when(ends)
    def _():
        pl.semaphore_wait(barrier, 1)

    @pl.when(jnp.logical_not(ends))
    def _():
        pl.semaphore_wait(barrier, 2)


def first_kernel(
    axis, count, pieces, hidden_ref, weight_ref, out_ref, weights, send, weight_sem, send_sem,
    recv_sem,
):
    me = lax.axis_index(axis)
    cols = weights.shape[2]
    last = count - 1

    def weight_copy(number, c):
        return pltpu.make_async_copy(
            weight_ref.at[:, pl.ds(pl.multiple_of(number * cols, cols), cols)],
            weights.at[c],
            weight_sem.at[c],
        )

    def copy(side, c, to):
        return pltpu.make_async_remote_copy(
            src_ref=send.at[c],
            dst_ref=out_ref.at[side, c],
            send_sem=send_sem.at[c],
            recv_sem=recv_sem.at[side, c],
            device_id={axis: to},
            device_id_type=MESH,
        )

    ends = jnp.logical_or(me == 0, me == last)

    @pl.when(ends)
    def _():
        pl.semaphore_wait(barrier, 1)

    @pl.when(jnp.logical_not(ends))
    def _():
        pl.semaphore_wait(barrier, 2)


def first_kernel(
    axis, count, pieces, hidden_ref, weight_ref, out_ref, weights, send, weight_sem, send_sem,
    recv_sem,
):
    me = lax.axis_index(axis)
    cols = weights.shape[2]
    last = count - 1

    def weight_copy(number, c):
        return pltpu.make_async_copy(
            weight_ref.at[:, pl.ds(pl.multiple_of(number * cols, cols), cols)],
            weights.at[c],
            weight_sem.at[c],
        )

    def copy(side, c, to):
        return pltpu.make_async_remote_copy(
            src_ref=send.at[c],
            dst_ref=out_ref.at[side, c],
            send_sem=send_sem.at[c],
            recv_sem=recv_sem.at[side, c],
            device_id={axis: to},
            device_id_type=MESH,
        )

    def run(side, chunk, to):
        for c in range(pieces):
            weight_copy(chunk * pieces + c, c).start()
        greet(axis, me, last)

        def piece(c, carry):
            weight_copy(chunk * pieces + c, c).wait()
            pack(
                send, c,
                jnp.dot(hidden_ref[...], weights[c], preferred_element_type=jnp.float32),
            )
            copy(side, c, to).start()
            return carry

        lax.fori_loop(0, pieces, piece, 0)
        for c in range(pieces):
            copy(side, c, to).wait_send()

    ends = jnp.logical_or(me == 0, me == last)
    side = jnp.where(me == 0, 0, 1)
    chunk = jnp.where(me == 0, last, 0)
    to = jnp.where(me == 0, 1, last - 1)

    @pl.when(ends)
    def _():
        for c in range(pieces):
            weight_copy(chunk * pieces + c, c).start()

    greet(axis, me, last)

    @pl.when(ends)
    def _():
        def piece(c, carry):
            weight_copy(chunk * pieces + c, c).wait()
            value = jnp.dot(hidden_ref[...], weights[c], preferred_element_type=jnp.float32)
            pack(send, c, value)
            copy(side, c, to).start()
            return carry

        lax.fori_loop(0, pieces, piece, 0)
        for c in range(pieces):
            copy(side, c, to).wait_send()

    @pl.when(me == 1)
    def _():
        for c in range(pieces):
            copy(0, c, 0).wait_recv()

    @pl.when(me == last - 1)
    def _():
        for c in range(pieces):
            copy(1, c, last).wait_recv()


def rest_kernel(
    axis, count, pieces, hidden_ref, weight_ref, first_ref, out_ref, weights, send, recv,
    weight_sem, first_sem, send_sem, recv_sem,
):
    me = lax.axis_index(axis)
    rows = hidden_ref.shape[0]
    cols = weights.shape[2]
    last = count - 1
    total = count * pieces

    def weight_copy(number):
        return pltpu.make_async_copy(
            weight_ref.at[:, pl.ds(pl.multiple_of(number * cols, cols), cols)],
            weights.at[number],
            weight_sem.at[number],
        )

    def first_copy(side, c):
        number = c if side else last * pieces + c
        return pltpu.make_async_copy(
            first_ref.at[side, c], recv.at[number], first_sem.at[side, c]
        )

    @pl.when(me == 1)
    def _():
        for c in range(pieces):
            first_copy(0, c).start()

    @pl.when(me == last - 1)
    def _():
        for c in range(pieces):
            first_copy(1, c).start()

    skip = jnp.where(jnp.logical_or(me == 0, me == last), pieces, 0)

    def fetch(i, carry):
        @pl.when(2 * me < count)
        def _():
            weight_copy(total - 1 - i).start()

        @pl.when(2 * me >= count)
        def _():
            weight_copy(i).start()

        return carry

    lax.fori_loop(skip, total, fetch, 0)
    greet(axis, me, last)

    def own(number):
        weight_copy(number).wait()
        return jnp.dot(hidden_ref[...], weights[number], preferred_element_type=jnp.float32)

    def copy(side, number, slot, c, to):
        return pltpu.make_async_remote_copy(
            src_ref=send.at[side * pieces + c],
            dst_ref=recv.at[slot],
            send_sem=send_sem.at[side, number],
            recv_sem=recv_sem.at[side, number],
            device_id={axis: to},
            device_id_type=MESH,
        )

    right = jnp.where(me == last, last - 1, me + 1)
    left = jnp.where(me == 0, 1, me - 1)

    def stage(step, carry):
        def piece(c, carry):
            number = (last - step + me) * pieces + c

            @pl.when(step >= me)
            def _():
                value = own(number)

                @pl.when(step > jnp.where(me == 0, 1, me))
                def _():
                    copy(0, number + pieces, number + pieces, c, right).wait_send()

                @pl.when(me == 0)
                def _():
                    pack(send, c, value)

                @pl.when(me > 0)
                def _():
                    @pl.when(jnp.logical_and(me == 1, step == 1))
                    def _():
                        pltpu.make_async_copy(
                            first_ref.at[0, c], recv.at[last * pieces + c], first_sem.at[0, c]
                        ).wait()

                    @pl.when(jnp.logical_not(jnp.logical_and(me == 1, step == 1)))
                    def _():
                        copy(0, number, number, c, right).wait_recv()

                    pack(send, c, value + unpack(recv, number, rows))

                copy(0, number, number, c, right).start()

            other = (step - last + me) * pieces + c

            @pl.when(step >= last - me)
            def _():
                value = own(other)

                @pl.when(step > jnp.where(me == last, 1, last - me))
                def _():
                    copy(1, other - pieces, other - pieces, c, left).wait_send()

                @pl.when(me == last)
                def _():
                    pack(send, pieces + c, value)

                @pl.when(me < last)
                def _():
                    @pl.when(jnp.logical_and(me == last - 1, step == 1))
                    def _():
                        pltpu.make_async_copy(
                            first_ref.at[1, c], recv.at[c], first_sem.at[1, c]
                        ).wait()

                    @pl.when(jnp.logical_not(jnp.logical_and(me == last - 1, step == 1)))
                    def _():
                        copy(1, other, other, c, left).wait_recv()

                    pack(send, pieces + c, value + unpack(recv, other, rows))

                slot = jnp.where(step == last - 1, total + c, other)
                copy(1, other, slot, c, left).start()

            return carry

        return lax.fori_loop(0, pieces, piece, carry)

    lax.fori_loop(1, last, stage, 0)

    def finish(c, carry):
        number = me * pieces + c
        out_ref[c] = own(number)

        @pl.when(me > 0)
        def _():
            copy(0, number, number, c, right).wait_recv()
            out_ref[c] = out_ref[c] + unpack(recv, number, rows)

        @pl.when(me < last)
        def _():
            copy(1, number, total + c, c, left).wait_recv()
            out_ref[c] = out_ref[c] + unpack(recv, total + c, rows)

        return carry

    lax.fori_loop(0, pieces, finish, 0)

    @pl.when(me < last)
    def _():
        for c in range(pieces):
            number = (me + 1) * pieces + c
            copy(0, number, number, c, right).wait_send()

    @pl.when(me > 0)
    def _():
        for c in range(pieces):
            number = (me - 1) * pieces + c
            copy(1, number, number, c, left).wait_send()


def base_parts(hidden, weight):
    rows, depth = hidden.shape
    count = lax.axis_size("tensor")
    width = weight.shape[1] // count
    pieces = max(1, width // 512)
    cols = width // pieces
    total = count * pieces
    vmem, hbm = pl.BlockSpec(memory_space=pltpu.VMEM), pl.BlockSpec(memory_space=pl.ANY)
    dma = pltpu.SemaphoreType.DMA

    def packed(number):
        return pltpu.VMEM((number, rows + 16, cols), jnp.int16)

    def params(number):
        return pltpu.CompilerParams(
            collective_id=number, has_side_effects=True, vmem_limit_bytes=58 * MIB
        )

    def cost(us):
        return pl.CostEstimate(flops=us * 1000000000, bytes_accessed=us * 1000000, transcendentals=0)

    def first():
        return pl.pallas_call(
            functools.partial(first_kernel, "tensor", count, pieces),
            out_shape=jax.ShapeDtypeStruct((2, pieces, rows + 16, cols), jnp.int16),
            in_specs=[vmem, hbm],
            out_specs=hbm,
            scratch_shapes=[
                pltpu.VMEM((pieces, depth, cols), jnp.bfloat16),
                packed(pieces),
                dma((pieces,)),
                dma((pieces,)),
                dma((2, pieces)),
            ],
            compiler_params=params(0),
            cost_estimate=cost(45),
        )(hidden, weight)

    def rest(got):
        return pl.pallas_call(
            functools.partial(rest_kernel, "tensor", count, pieces),
            out_shape=jax.ShapeDtypeStruct((pieces, rows, cols), jnp.float32),
            in_specs=[vmem, hbm, hbm],
            out_specs=vmem,
            scratch_shapes=[
                pltpu.VMEM((total, depth, cols), jnp.bfloat16),
                packed(2 * pieces),
                packed(total + pieces),
                dma((total,)),
                dma((2, pieces)),
                dma((2, total)),
                dma((2, total)),
            ],
            compiler_params=params(1),
            cost_estimate=cost(90),
        )(hidden, weight, got)

    return first, rest


def shift(x, by, count):
    return lax.ppermute(x, "dp", [(i, (i + by) % count) for i in range(count)])


def per_device(
    hidden, output_weight, adapter_down_maps, adapter_up_maps, adapter_slot, segment_adapter
):
    rows, width = hidden.shape
    segs = segment_adapter.shape[0]
    block = rows // segs
    stored, rank_dim, _ = adapter_down_maps.shape
    dp = lax.axis_size("dp")
    me = lax.axis_index("dp")
    cap = segs // 2
    slot = adapter_slot[segment_adapter]
    rel = (slot // stored - me) % dp
    local = slot % stored
    mask = rel[None, :] == jnp.arange(dp, dtype=jnp.int32)[:, None]
    running = jnp.cumsum(mask.astype(jnp.int32), axis=1) - 1
    position = jnp.sum(jnp.where(mask, running, 0), axis=0)
    match = mask[:, None, :] & (
        position[None, None, :] == jnp.arange(cap, dtype=jnp.int32)[None, :, None]
    )
    picked = jnp.sum(
        jnp.where(match, jnp.arange(segs, dtype=jnp.int32)[None, None, :], 0), axis=2
    )
    wanted = jnp.sum(jnp.where(match, local[None, None, :], 0), axis=2)
    place = rel * cap + position
    seg_rows = hidden.reshape(segs, block, width)
    out_rows = seg_rows[picked]
    got_slots = [wanted[0]] + [shift(wanted[k], k, dp) for k in range(1, dp)]
    got_rows = [out_rows[0]] + [shift(out_rows[k], k, dp) for k in range(1, dp)]
    slots = jnp.concatenate(got_slots)
    there_rows = jnp.concatenate(got_rows)
    first, rest = base_parts(hidden, output_weight)
    part, there_rows = lax.optimization_barrier((first(), there_rows))
    rank = apply_maps(down_kernel, slots, there_rows, adapter_down_maps, (block, rank_dim))
    rank = lax.psum(rank, "tensor")
    delta = apply_maps(up_kernel, slots, rank, adapter_up_maps, (block, width))
    part, delta = lax.optimization_barrier((part, delta))
    delta = delta.reshape(dp, cap, block, width)
    back = [delta[0]] + [shift(delta[k], dp - k, dp) for k in range(1, dp)]
    delta_rows = jnp.concatenate(back)[place].reshape(rows, width)
    base = rest(part).transpose(1, 0, 2).reshape(rows, width)
    return (base + delta_rows).astype(jnp.bfloat16)


def solution(mesh):
    return jax.shard_map(
        per_device,
        mesh=mesh,
        in_specs=(
            P(("groups", "dp"), "tensor"),
            P("tensor", None),
            P("dp", None, "tensor"),
            P("dp", None, "tensor"),
            P("groups"),
            P(("groups", "dp")),
        ),
        out_specs=P(("groups", "dp"), "tensor"),
        check_vma=False,
    )
```

```python
import functools

import jax
import jax.numpy as jnp
from jax import lax
from jax.experimental import pallas as pl
from jax.experimental.pallas import tpu as pltpu
from jax.sharding import PartitionSpec as P

MIB = 1024 * 1024
STEP = 8


def down_kernel(step, slots_ref, rows_ref, *refs):
    maps, out_ref = refs[:step], refs[step]
    for i in range(0, step, 2):
        out_ref[i // 2] = jnp.concatenate(
            [
                lax.dot_general(
                    rows_ref[j], maps[j][0], (((1,), (1,)), ((), ())),
                    preferred_element_type=jnp.float32,
                )
                for j in (i, i + 1)
            ],
            axis=1,
        )


def up_kernel(step, slots_ref, rank_ref, *refs):
    maps, out_ref = refs[:step], refs[step]
    for i in range(step):
        pair = rank_ref[i // 2]
        block, half = pair.shape[0], pair.shape[1] // 2
        rank = pair[:, (i % 2) * half:(i % 2 + 1) * half]
        high = rank.astype(jnp.bfloat16)
        rest = rank - high.astype(jnp.float32)
        mid = rest.astype(jnp.bfloat16)
        low = (rest - mid.astype(jnp.float32)).astype(jnp.bfloat16)
        parts = jnp.concatenate([high, mid, low], axis=0)
        got = jnp.dot(parts, maps[i][0], preferred_element_type=jnp.float32)
        out_ref[i] = (got[2 * block:] + got[block:2 * block]) + got[:block]


def map_specs(step, maps):
    shape = (1,) + maps.shape[1:]

    def spec(i):
        return pl.BlockSpec(shape, lambda g, slots: (slots[g * step + i], 0, 0))

    return [spec(i) for i in range(step)]


def apply_maps(kernel, slots, values, maps, out_tail, fold_in, fold_out):
    count = slots.shape[0]
    step = STEP if count % STEP == 0 else 2
    tail = values.shape[1:]
    return pl.pallas_call(
        functools.partial(kernel, step),
        grid_spec=pltpu.PrefetchScalarGridSpec(
            num_scalar_prefetch=1,
            grid=(count // step,),
            in_specs=[pl.BlockSpec((step // fold_in,) + tail, lambda g, slots: (g, 0, 0))]
            + map_specs(step, maps),
            out_specs=pl.BlockSpec((step // fold_out,) + out_tail, lambda g, slots: (g, 0, 0)),
        ),
        out_shape=jax.ShapeDtypeStruct((count // fold_out,) + out_tail, jnp.float32),
        compiler_params=pltpu.CompilerParams(vmem_limit_bytes=40 * MIB),
    )(slots, values, *([maps] * step))


FINE = 128.0
TOP = 32767.0
MESH = pl.DeviceIdType.MESH


def pack(ref, at, value):
    rows, cols = value.shape
    top = jnp.maximum(jnp.max(jnp.abs(value), axis=0, keepdims=True), 1e-30)
    code = jnp.ceil(jnp.log2(top) * FINE + 0.125)
    scale = jnp.exp2(code * (1.0 / FINE))
    whole = jnp.round(jnp.clip(value * (TOP / scale), -TOP, TOP))
    ref[at, :rows, :] = whole.astype(jnp.int32).astype(jnp.int16)
    ref[at, rows:, :] = jnp.broadcast_to(code.astype(jnp.int32), (16, cols)).astype(jnp.int16)


def unpack(ref, at, rows):
    code = ref[at, rows:, :].astype(jnp.int32).astype(jnp.float32)[:1]
    scale = jnp.exp2(code * (1.0 / FINE)) * (1.0 / TOP)
    return ref[at, :rows, :].astype(jnp.int32).astype(jnp.float32) * scale


def greet(axis, me, last):
    barrier = pltpu.get_barrier_semaphore()

    @pl.when(me > 0)
    def _():
        pl.semaphore_signal(barrier, inc=1, device_id={axis: me - 1}, device_id_type=MESH)

    @pl.when(me < last)
    def _():
        pl.semaphore_signal(barrier, inc=1, device_id={axis: me + 1}, device_id_type=MESH)

    ends = jnp.logical_or(me == 0, me == last)

    @pl.when(ends)
    def _():
        pl.semaphore_wait(barrier, 1)

    @pl.when(jnp.logical_not(ends))
    def _():
        pl.semaphore_wait(barrier, 2)


def first_kernel(
    axis, count, pieces, hidden_ref, weight_ref, out_ref, weights, send, weight_sem, send_sem,
    recv_sem,
):
    me = lax.axis_index(axis)
    cols = weights.shape[2]
    last = count - 1

    def weight_copy(number, c):
        return pltpu.make_async_copy(
            weight_ref.at[:, pl.ds(pl.multiple_of(number * cols, cols), cols)],
            weights.at[c],
            weight_sem.at[c],
        )

    def copy(side, c, to):
        return pltpu.make_async_remote_copy(
            src_ref=send.at[c],
            dst_ref=out_ref.at[side, c],
            send_sem=send_sem.at[c],
            recv_sem=recv_sem.at[side, c],
            device_id={axis: to},
            device_id_type=MESH,
        )

    ends = jnp.logical_or(me == 0, me == last)

    @pl.when(ends)
    def _():
        pl.semaphore_wait(barrier, 1)

    @pl.when(jnp.logical_not(ends))
    def _():
        pl.semaphore_wait(barrier, 2)


def first_kernel(
    axis, count, pieces, hidden_ref, weight_ref, out_ref, weights, send, weight_sem, send_sem,
    recv_sem,
):
    me = lax.axis_index(axis)
    cols = weights.shape[2]
    last = count - 1

    def weight_copy(number, c):
        return pltpu.make_async_copy(
            weight_ref.at[:, pl.ds(pl.multiple_of(number * cols, cols), cols)],
            weights.at[c],
            weight_sem.at[c],
        )

    def copy(side, c, to):
        return pltpu.make_async_remote_copy(
            src_ref=send.at[c],
            dst_ref=out_ref.at[side, c],
            send_sem=send_sem.at[c],
            recv_sem=recv_sem.at[side, c],
            device_id={axis: to},
            device_id_type=MESH,
        )

    def run(side, chunk, to):
        for c in range(pieces):
            weight_copy(chunk * pieces + c, c).start()
        greet(axis, me, last)

        def piece(c, carry):
            weight_copy(chunk * pieces + c, c).wait()
            pack(
                send, c,
                jnp.dot(hidden_ref[...], weights[c], preferred_element_type=jnp.float32),
            )
            copy(side, c, to).start()
            return carry

        lax.fori_loop(0, pieces, piece, 0)
        for c in range(pieces):
            copy(side, c, to).wait_send()

    ends = jnp.logical_or(me == 0, me == last)
    side = jnp.where(me == 0, 0, 1)
    chunk = jnp.where(me == 0, last, 0)
    to = jnp.where(me == 0, 1, last - 1)

    @pl.when(ends)
    def _():
        for c in range(pieces):
            weight_copy(chunk * pieces + c, c).start()

    greet(axis, me, last)

    @pl.when(ends)
    def _():
        def piece(c, carry):
            weight_copy(chunk * pieces + c, c).wait()
            value = jnp.dot(hidden_ref[...], weights[c], preferred_element_type=jnp.float32)
            pack(send, c, value)
            copy(side, c, to).start()
            return carry

        lax.fori_loop(0, pieces, piece, 0)
        for c in range(pieces):
            copy(side, c, to).wait_send()

    @pl.when(me == 1)
    def _():
        for c in range(pieces):
            copy(0, c, 0).wait_recv()

    @pl.when(me == last - 1)
    def _():
        for c in range(pieces):
            copy(1, c, last).wait_recv()


def rest_kernel(
    axis, count, pieces, hidden_ref, weight_ref, first_ref, out_ref, weights, send, recv,
    weight_sem, first_sem, send_sem, recv_sem,
):
    me = lax.axis_index(axis)
    rows = hidden_ref.shape[0]
    cols = weights.shape[2]
    last = count - 1
    total = count * pieces

    def weight_copy(number):
        return pltpu.make_async_copy(
            weight_ref.at[:, pl.ds(pl.multiple_of(number * cols, cols), cols)],
            weights.at[number],
            weight_sem.at[number],
        )

    def first_copy(side, c):
        number = c if side else last * pieces + c
        return pltpu.make_async_copy(
            first_ref.at[side, c], recv.at[number], first_sem.at[side, c]
        )

    @pl.when(me == 1)
    def _():
        for c in range(pieces):
            first_copy(0, c).start()

    @pl.when(me == last - 1)
    def _():
        for c in range(pieces):
            first_copy(1, c).start()

    skip = jnp.where(jnp.logical_or(me == 0, me == last), pieces, 0)

    def fetch(i, carry):
        @pl.when(2 * me < count)
        def _():
            weight_copy(total - 1 - i).start()

        @pl.when(2 * me >= count)
        def _():
            weight_copy(i).start()

        return carry

    lax.fori_loop(skip, total, fetch, 0)
    greet(axis, me, last)

    def own(number):
        weight_copy(number).wait()
        return jnp.dot(hidden_ref[...], weights[number], preferred_element_type=jnp.float32)

    def copy(side, number, slot, c, to):
        return pltpu.make_async_remote_copy(
            src_ref=send.at[side * pieces + c],
            dst_ref=recv.at[slot],
            send_sem=send_sem.at[side, number],
            recv_sem=recv_sem.at[side, number],
            device_id={axis: to},
            device_id_type=MESH,
        )

    right = jnp.where(me == last, last - 1, me + 1)
    left = jnp.where(me == 0, 1, me - 1)

    def stage(step, carry):
        def piece(c, carry):
            number = (last - step + me) * pieces + c

            @pl.when(step >= me)
            def _():
                value = own(number)

                @pl.when(step > jnp.where(me == 0, 1, me))
                def _():
                    copy(0, number + pieces, number + pieces, c, right).wait_send()

                @pl.when(me == 0)
                def _():
                    pack(send, c, value)

                @pl.when(me > 0)
                def _():
                    @pl.when(jnp.logical_and(me == 1, step == 1))
                    def _():
                        pltpu.make_async_copy(
                            first_ref.at[0, c], recv.at[last * pieces + c], first_sem.at[0, c]
                        ).wait()

                    @pl.when(jnp.logical_not(jnp.logical_and(me == 1, step == 1)))
                    def _():
                        copy(0, number, number, c, right).wait_recv()

                    pack(send, c, value + unpack(recv, number, rows))

                copy(0, number, number, c, right).start()

            other = (step - last + me) * pieces + c

            @pl.when(step >= last - me)
            def _():
                value = own(other)

                @pl.when(step > jnp.where(me == last, 1, last - me))
                def _():
                    copy(1, other - pieces, other - pieces, c, left).wait_send()

                @pl.when(me == last)
                def _():
                    pack(send, pieces + c, value)

                @pl.when(me < last)
                def _():
                    @pl.when(jnp.logical_and(me == last - 1, step == 1))
                    def _():
                        pltpu.make_async_copy(
                            first_ref.at[1, c], recv.at[c], first_sem.at[1, c]
                        ).wait()

                    @pl.when(jnp.logical_not(jnp.logical_and(me == last - 1, step == 1)))
                    def _():
                        copy(1, other, other, c, left).wait_recv()

                    pack(send, pieces + c, value + unpack(recv, other, rows))

                slot = jnp.where(step == last - 1, total + c, other)
                copy(1, other, slot, c, left).start()

            return carry

        return lax.fori_loop(0, pieces, piece, carry)

    lax.fori_loop(1, last, stage, 0)

    def finish(c, carry):
        number = me * pieces + c
        out_ref[c] = own(number)

        @pl.when(me > 0)
        def _():
            copy(0, number, number, c, right).wait_recv()
            out_ref[c] = out_ref[c] + unpack(recv, number, rows)

        @pl.when(me < last)
        def _():
            copy(1, number, total + c, c, left).wait_recv()
            out_ref[c] = out_ref[c] + unpack(recv, total + c, rows)

        return carry

    lax.fori_loop(0, pieces, finish, 0)

    @pl.when(me < last)
    def _():
        for c in range(pieces):
            number = (me + 1) * pieces + c
            copy(0, number, number, c, right).wait_send()

    @pl.when(me > 0)
    def _():
        for c in range(pieces):
            number = (me - 1) * pieces + c
            copy(1, number, number, c, left).wait_send()


def base_parts(hidden, weight):
    rows, depth = hidden.shape
    count = lax.axis_size("tensor")
    width = weight.shape[1] // count
    pieces = max(1, width // 512)
    cols = width // pieces
    total = count * pieces
    vmem, hbm = pl.BlockSpec(memory_space=pltpu.VMEM), pl.BlockSpec(memory_space=pl.ANY)
    dma = pltpu.SemaphoreType.DMA

    def packed(number):
        return pltpu.VMEM((number, rows + 16, cols), jnp.int16)

    def params(number):
        return pltpu.CompilerParams(
            collective_id=number, has_side_effects=True, vmem_limit_bytes=58 * MIB
        )

    def cost(us):
        return pl.CostEstimate(flops=us * 1000000000, bytes_accessed=us * 1000000, transcendentals=0)

    def first():
        return pl.pallas_call(
            functools.partial(first_kernel, "tensor", count, pieces),
            out_shape=jax.ShapeDtypeStruct((2, pieces, rows + 16, cols), jnp.int16),
            in_specs=[vmem, hbm],
            out_specs=hbm,
            scratch_shapes=[
                pltpu.VMEM((pieces, depth, cols), jnp.bfloat16),
                packed(pieces),
                dma((pieces,)),
                dma((pieces,)),
                dma((2, pieces)),
            ],
            compiler_params=params(0),
            cost_estimate=cost(45),
        )(hidden, weight)

    def rest(got):
        return pl.pallas_call(
            functools.partial(rest_kernel, "tensor", count, pieces),
            out_shape=jax.ShapeDtypeStruct((pieces, rows, cols), jnp.float32),
            in_specs=[vmem, hbm, hbm],
            out_specs=vmem,
            scratch_shapes=[
                pltpu.VMEM((total, depth, cols), jnp.bfloat16),
                packed(2 * pieces),
                packed(total + pieces),
                dma((total,)),
                dma((2, pieces)),
                dma((2, total)),
                dma((2, total)),
            ],
            compiler_params=params(1),
            cost_estimate=cost(90),
        )(hidden, weight, got)

    return first, rest


def sum_kernel(axis, count, in_ref, out_ref, parts, full, send_sem, recv_sem):
    me = lax.axis_index(axis)
    size = parts.shape[1]

    def peer(k):
        return lax.rem(me + k, count)

    barrier = pltpu.get_barrier_semaphore()
    for k in range(1, count):
        pl.semaphore_signal(barrier, inc=1, device_id={axis: peer(k)}, device_id_type=MESH)
    pl.semaphore_wait(barrier, count - 1)

    def scatter(k):
        return pltpu.make_async_remote_copy(
            src_ref=in_ref.at[pl.ds(peer(k) * size, size)],
            dst_ref=parts.at[k],
            send_sem=send_sem.at[0, k],
            recv_sem=recv_sem.at[0, k],
            device_id={axis: peer(k)},
            device_id_type=MESH,
        )

    def gather(k):
        mine = full.at[pl.ds(me * size, size)]
        return pltpu.make_async_remote_copy(
            src_ref=mine,
            dst_ref=mine,
            send_sem=send_sem.at[1, k],
            recv_sem=recv_sem.at[1, k],
            device_id={axis: peer(k)},
            device_id_type=MESH,
        )

    for k in range(1, count):
        scatter(k).start()
    total = in_ref[pl.ds(me * size, size)]
    for k in range(1, count):
        scatter(k).wait_recv()
        total = total + parts[k]
    full[pl.ds(me * size, size)] = total
    for k in range(1, count):
        gather(k).start()
    for k in range(1, count):
        gather(k).wait_recv()
    out_ref[...] = full[...]
    for k in range(1, count):
        scatter(k).wait_send()
        gather(k).wait_send()


def sum_over_tensor(x):
    count = lax.axis_size("tensor")
    size = x.shape[0] // count
    vmem = pl.BlockSpec(memory_space=pltpu.VMEM)
    return pl.pallas_call(
        functools.partial(sum_kernel, "tensor", count),
        out_shape=jax.ShapeDtypeStruct(x.shape, x.dtype),
        in_specs=[vmem],
        out_specs=vmem,
        scratch_shapes=[
            pltpu.VMEM((count, size) + x.shape[1:], x.dtype),
            pltpu.VMEM(x.shape, x.dtype),
            pltpu.SemaphoreType.DMA((2, count)),
            pltpu.SemaphoreType.DMA((2, count)),
        ],
        compiler_params=pltpu.CompilerParams(
            collective_id=2, has_side_effects=True, vmem_limit_bytes=16 * MIB
        ),
    )(x)


def join_kernel(held_ref, rel_ref, base_ref, *refs):
    deltas, out_ref = refs[:-1], refs[-1]
    pieces, _, cols = base_ref.shape
    for k, delta in enumerate(deltas):
        @pl.when(rel_ref[pl.program_id(0)] == k)
        def _():
            for c in range(pieces):
                part = slice(c * cols, (c + 1) * cols)
                out_ref[:, part] = (base_ref[c] + delta[0, :, part]).astype(out_ref.dtype)


def join(base, deltas, held, rel):
    pieces, rows, cols = base.shape
    segs = rel.shape[0]
    _, block, width = deltas[0].shape

    def spec(k):
        return pl.BlockSpec((1, block, width), lambda s, held, rel: (held[k * segs + s], 0, 0))

    return pl.pallas_call(
        join_kernel,
        grid_spec=pltpu.PrefetchScalarGridSpec(
            num_scalar_prefetch=2,
            grid=(segs,),
            in_specs=[pl.BlockSpec((pieces, block, cols), lambda s, held, rel: (0, s, 0))]
            + [spec(k) for k in range(len(deltas))],
            out_specs=pl.BlockSpec((block, width), lambda s, held, rel: (s, 0)),
        ),
        out_shape=jax.ShapeDtypeStruct((rows, width), jnp.bfloat16),
        compiler_params=pltpu.CompilerParams(vmem_limit_bytes=16 * MIB),
    )(held, rel, base, *deltas)


def shift(x, by, count):
    return lax.ppermute(x, "dp", [(i, (i + by) % count) for i in range(count)])


def per_device(
    hidden, output_weight, adapter_down_maps, adapter_up_maps, adapter_slot, segment_adapter
):
    rows, width = hidden.shape
    segs = segment_adapter.shape[0]
    block = rows // segs
    stored, rank_dim, _ = adapter_down_maps.shape
    dp = lax.axis_size("dp")
    me = lax.axis_index("dp")
    cap = segs // 2
    slot = adapter_slot[segment_adapter]
    rel = (slot // stored - me) % dp
    local = slot % stored
    mask = rel[None, :] == jnp.arange(dp, dtype=jnp.int32)[:, None]
    running = jnp.cumsum(mask.astype(jnp.int32), axis=1) - 1
    position = jnp.sum(jnp.where(mask, running, 0), axis=0)
    match = mask[:, None, :] & (
        position[None, None, :] == jnp.arange(cap, dtype=jnp.int32)[None, :, None]
    )
    picked = jnp.sum(
        jnp.where(match, jnp.arange(segs, dtype=jnp.int32)[None, None, :], 0), axis=2
    )
    wanted = jnp.sum(jnp.where(match, local[None, None, :], 0), axis=2)
    held = jnp.clip(running, 0, cap - 1).astype(jnp.int32).reshape(-1)
    seg_rows = hidden.reshape(segs, block, width)
    out_rows = seg_rows[picked]
    got_slots = [wanted[0]] + [shift(wanted[k], k, dp) for k in range(1, dp)]
    got_rows = [out_rows[0]] + [shift(out_rows[k], k, dp) for k in range(1, dp)]
    slots = jnp.concatenate(got_slots)
    there_rows = jnp.concatenate(got_rows)
    first, rest = base_parts(hidden, output_weight)
    part, there_rows = lax.optimization_barrier((first(), there_rows))
    rank = apply_maps(down_kernel, slots, there_rows, adapter_down_maps, (block, 2 * rank_dim), 1, 2)
    rank = sum_over_tensor(rank)
    delta = apply_maps(up_kernel, slots, rank, adapter_up_maps, (block, width), 2, 1)
    part, delta = lax.optimization_barrier((part, delta))
    delta = delta.reshape(dp, cap, block, width)
    back = [delta[0]] + [shift(delta[k], dp - k, dp) for k in range(1, dp)]
    return join(rest(part), back, held, rel.astype(jnp.int32))


def solution(mesh):
    return jax.shard_map(
        per_device,
        mesh=mesh,
        in_specs=(
            P(("groups", "dp"), "tensor"),
            P("tensor", None),
            P("dp", None, "tensor"),
            P("dp", None, "tensor"),
            P("groups"),
            P(("groups", "dp")),
        ),
        out_specs=P(("groups", "dp"), "tensor"),
        check_vma=False,
    )
```

```python
import functools

import jax
import jax.numpy as jnp
from jax import lax
from jax.experimental import pallas as pl
from jax.experimental.pallas import tpu as pltpu
from jax.sharding import PartitionSpec as P

MIB = 1024 * 1024
STEP = 8
PAIR = 2


def down_kernel(step, slots_ref, rows_ref, *refs):
    maps, out_ref = refs[:step], refs[step]
    for i in range(0, step, 2):
        out_ref[i // 2] = jnp.concatenate(
            [
                lax.dot_general(
                    rows_ref[j], maps[j][0], (((1,), (1,)), ((), ())),
                    preferred_element_type=jnp.float32,
                )
                for j in (i, i + 1)
            ],
            axis=1,
        )


def up_kernel(step, slots_ref, rank_ref, *refs):
    maps, out_ref = refs[:step], refs[step]
    for i in range(step):
        pair = rank_ref[i // 2]
        block, half = pair.shape[0], pair.shape[1] // 2
        rank = pair[:, (i % 2) * half:(i % 2 + 1) * half]
        high = rank.astype(jnp.bfloat16)
        rest = rank - high.astype(jnp.float32)
        mid = rest.astype(jnp.bfloat16)
        low = (rest - mid.astype(jnp.float32)).astype(jnp.bfloat16)
        parts = jnp.concatenate([high, mid, low], axis=0)
        got = jnp.dot(parts, maps[i][0], preferred_element_type=jnp.float32)
        out_ref[i] = (got[2 * block:] + got[block:2 * block]) + got[:block]


def map_specs(step, maps):
    shape = (1,) + maps.shape[1:]

    def spec(i):
        return pl.BlockSpec(shape, lambda g, slots: (slots[g * step + i], 0, 0))

    return [spec(i) for i in range(step)]


def apply_maps(kernel, slots, values, maps, out_tail, fold_in, fold_out):
    count = slots.shape[0]
    step = STEP if count % STEP == 0 else 2
    tail = values.shape[1:]
    return pl.pallas_call(
        functools.partial(kernel, step),
        grid_spec=pltpu.PrefetchScalarGridSpec(
            num_scalar_prefetch=1,
            grid=(count // step,),
            in_specs=[pl.BlockSpec((step // fold_in,) + tail, lambda g, slots: (g, 0, 0))]
            + map_specs(step, maps),
            out_specs=pl.BlockSpec((step // fold_out,) + out_tail, lambda g, slots: (g, 0, 0)),
        ),
        out_shape=jax.ShapeDtypeStruct((count // fold_out,) + out_tail, jnp.float32),
        compiler_params=pltpu.CompilerParams(vmem_limit_bytes=40 * MIB),
    )(slots, values, *([maps] * step))


FINE = 128.0
TOP = 32767.0
MESH = pl.DeviceIdType.MESH


def pack(ref, at, value):
    rows, cols = value.shape
    top = jnp.maximum(jnp.max(jnp.abs(value), axis=0, keepdims=True), 1e-30)
    code = jnp.ceil(jnp.log2(top) * FINE + 0.125)
    scale = jnp.exp2(code * (1.0 / FINE))
    whole = jnp.round(jnp.clip(value * (TOP / scale), -TOP, TOP))
    ref[at, :rows, :] = whole.astype(jnp.int32).astype(jnp.int16)
    ref[at, rows:, :] = jnp.broadcast_to(code.astype(jnp.int32), (16, cols)).astype(jnp.int16)


def unpack(ref, at, rows):
    code = ref[at, rows:, :].astype(jnp.int32).astype(jnp.float32)[:1]
    scale = jnp.exp2(code * (1.0 / FINE)) * (1.0 / TOP)
    return ref[at, :rows, :].astype(jnp.int32).astype(jnp.float32) * scale


def greet(axis, me, last):
    barrier = pltpu.get_barrier_semaphore()

    @pl.when(me > 0)
    def _():
        pl.semaphore_signal(barrier, inc=1, device_id={axis: me - 1}, device_id_type=MESH)

    @pl.when(me < last)
    def _():
        pl.semaphore_signal(barrier, inc=1, device_id={axis: me + 1}, device_id_type=MESH)

    ends = jnp.logical_or(me == 0, me == last)

    @pl.when(ends)
    def _():
        pl.semaphore_wait(barrier, 1)

    @pl.when(jnp.logical_not(ends))
    def _():
        pl.semaphore_wait(barrier, 2)


def first_kernel(
    axis, count, pieces, hidden_ref, weight_ref, out_ref, weights, send, weight_sem, send_sem,
    recv_sem,
):
    me = lax.axis_index(axis)
    cols = weights.shape[2]
    last = count - 1

    def weight_copy(number, c):
        return pltpu.make_async_copy(
            weight_ref.at[:, pl.ds(pl.multiple_of(number * cols, cols), cols)],
            weights.at[c],
            weight_sem.at[c],
        )

    def copy(side, c, to):
        return pltpu.make_async_remote_copy(
            src_ref=send.at[c],
            dst_ref=out_ref.at[side, c],
            send_sem=send_sem.at[c],
            recv_sem=recv_sem.at[side, c],
            device_id={axis: to},
            device_id_type=MESH,
        )

    ends = jnp.logical_or(me == 0, me == last)

    @pl.when(ends)
    def _():
        pl.semaphore_wait(barrier, 1)

    @pl.when(jnp.logical_not(ends))
    def _():
        pl.semaphore_wait(barrier, 2)


def first_kernel(
    axis, count, pieces, hidden_ref, weight_ref, out_ref, weights, send, weight_sem, send_sem,
    recv_sem,
):
    me = lax.axis_index(axis)
    cols = weights.shape[2]
    last = count - 1

    def weight_copy(number, c):
        return pltpu.make_async_copy(
            weight_ref.at[:, pl.ds(pl.multiple_of(number * cols, cols), cols)],
            weights.at[c],
            weight_sem.at[c],
        )

    def copy(side, c, to):
        return pltpu.make_async_remote_copy(
            src_ref=send.at[c],
            dst_ref=out_ref.at[side, c],
            send_sem=send_sem.at[c],
            recv_sem=recv_sem.at[side, c],
            device_id={axis: to},
            device_id_type=MESH,
        )

    def run(side, chunk, to):
        for c in range(pieces):
            weight_copy(chunk * pieces + c, c).start()
        greet(axis, me, last)

        def piece(c, carry):
            weight_copy(chunk * pieces + c, c).wait()
            pack(
                send, c,
                jnp.dot(hidden_ref[...], weights[c], preferred_element_type=jnp.float32),
            )
            copy(side, c, to).start()
            return carry

        lax.fori_loop(0, pieces, piece, 0)
        for c in range(pieces):
            copy(side, c, to).wait_send()

    ends = jnp.logical_or(me == 0, me == last)
    side = jnp.where(me == 0, 0, 1)
    chunk = jnp.where(me == 0, last, 0)
    to = jnp.where(me == 0, 1, last - 1)

    @pl.when(ends)
    def _():
        for c in range(pieces):
            weight_copy(chunk * pieces + c, c).start()

    greet(axis, me, last)

    @pl.when(ends)
    def _():
        def piece(c, carry):
            weight_copy(chunk * pieces + c, c).wait()
            value = jnp.dot(hidden_ref[...], weights[c], preferred_element_type=jnp.float32)
            pack(send, c, value)
            copy(side, c, to).start()
            return carry

        lax.fori_loop(0, pieces, piece, 0)
        for c in range(pieces):
            copy(side, c, to).wait_send()

    @pl.when(me == 1)
    def _():
        for c in range(pieces):
            copy(0, c, 0).wait_recv()

    @pl.when(me == last - 1)
    def _():
        for c in range(pieces):
            copy(1, c, last).wait_recv()


def rest_kernel(
    axis, count, pieces, hidden_ref, weight_ref, first_ref, out_ref, weights, send, recv,
    weight_sem, first_sem, send_sem, recv_sem,
):
    me = lax.axis_index(axis)
    rows = hidden_ref.shape[0]
    cols = weights.shape[2]
    last = count - 1
    total = count * pieces

    def weight_copy(number):
        return pltpu.make_async_copy(
            weight_ref.at[:, pl.ds(pl.multiple_of(number * cols, cols), cols)],
            weights.at[number],
            weight_sem.at[number],
        )

    def first_copy(side, c):
        number = c if side else last * pieces + c
        return pltpu.make_async_copy(
            first_ref.at[side, c], recv.at[number], first_sem.at[side, c]
        )

    @pl.when(me == 1)
    def _():
        for c in range(pieces):
            first_copy(0, c).start()

    @pl.when(me == last - 1)
    def _():
        for c in range(pieces):
            first_copy(1, c).start()

    skip = jnp.where(jnp.logical_or(me == 0, me == last), pieces, 0)

    def fetch(i, carry):
        @pl.when(2 * me < count)
        def _():
            weight_copy(total - 1 - i).start()

        @pl.when(2 * me >= count)
        def _():
            weight_copy(i).start()

        return carry

    lax.fori_loop(skip, total, fetch, 0)
    greet(axis, me, last)

    def own(number):
        weight_copy(number).wait()
        return jnp.dot(hidden_ref[...], weights[number], preferred_element_type=jnp.float32)

    def copy(side, number, slot, c, to):
        return pltpu.make_async_remote_copy(
            src_ref=send.at[side * pieces + c],
            dst_ref=recv.at[slot],
            send_sem=send_sem.at[side, number],
            recv_sem=recv_sem.at[side, number],
            device_id={axis: to},
            device_id_type=MESH,
        )

    right = jnp.where(me == last, last - 1, me + 1)
    left = jnp.where(me == 0, 1, me - 1)

    def stage(step, carry):
        def piece(c, carry):
            number = (last - step + me) * pieces + c

            @pl.when(step >= me)
            def _():
                value = own(number)

                @pl.when(step > jnp.where(me == 0, 1, me))
                def _():
                    copy(0, number + pieces, number + pieces, c, right).wait_send()

                @pl.when(me == 0)
                def _():
                    pack(send, c, value)

                @pl.when(me > 0)
                def _():
                    @pl.when(jnp.logical_and(me == 1, step == 1))
                    def _():
                        pltpu.make_async_copy(
                            first_ref.at[0, c], recv.at[last * pieces + c], first_sem.at[0, c]
                        ).wait()

                    @pl.when(jnp.logical_not(jnp.logical_and(me == 1, step == 1)))
                    def _():
                        copy(0, number, number, c, right).wait_recv()

                    pack(send, c, value + unpack(recv, number, rows))

                copy(0, number, number, c, right).start()

            other = (step - last + me) * pieces + c

            @pl.when(step >= last - me)
            def _():
                value = own(other)

                @pl.when(step > jnp.where(me == last, 1, last - me))
                def _():
                    copy(1, other - pieces, other - pieces, c, left).wait_send()

                @pl.when(me == last)
                def _():
                    pack(send, pieces + c, value)

                @pl.when(me < last)
                def _():
                    @pl.when(jnp.logical_and(me == last - 1, step == 1))
                    def _():
                        pltpu.make_async_copy(
                            first_ref.at[1, c], recv.at[c], first_sem.at[1, c]
                        ).wait()

                    @pl.when(jnp.logical_not(jnp.logical_and(me == last - 1, step == 1)))
                    def _():
                        copy(1, other, other, c, left).wait_recv()

                    pack(send, pieces + c, value + unpack(recv, other, rows))

                slot = jnp.where(step == last - 1, total + c, other)
                copy(1, other, slot, c, left).start()

            return carry

        return lax.fori_loop(0, pieces, piece, carry)

    lax.fori_loop(1, last, stage, 0)

    def finish(c, carry):
        number = me * pieces + c
        out_ref[c] = own(number)

        @pl.when(me > 0)
        def _():
            copy(0, number, number, c, right).wait_recv()
            out_ref[c] = out_ref[c] + unpack(recv, number, rows)

        @pl.when(me < last)
        def _():
            copy(1, number, total + c, c, left).wait_recv()
            out_ref[c] = out_ref[c] + unpack(recv, total + c, rows)

        return carry

    lax.fori_loop(0, pieces, finish, 0)

    @pl.when(me < last)
    def _():
        for c in range(pieces):
            number = (me + 1) * pieces + c
            copy(0, number, number, c, right).wait_send()

    @pl.when(me > 0)
    def _():
        for c in range(pieces):
            number = (me - 1) * pieces + c
            copy(1, number, number, c, left).wait_send()


def base_parts(hidden, weight):
    rows, depth = hidden.shape
    count = lax.axis_size("tensor")
    width = weight.shape[1] // count
    pieces = max(1, width // 512)
    cols = width // pieces
    total = count * pieces
    vmem, hbm = pl.BlockSpec(memory_space=pltpu.VMEM), pl.BlockSpec(memory_space=pl.ANY)
    dma = pltpu.SemaphoreType.DMA

    def packed(number):
        return pltpu.VMEM((number, rows + 16, cols), jnp.int16)

    def params(number):
        return pltpu.CompilerParams(
            collective_id=number, has_side_effects=True, vmem_limit_bytes=58 * MIB
        )

    def cost(us):
        return pl.CostEstimate(flops=us * 1000000000, bytes_accessed=us * 1000000, transcendentals=0)

    def first():
        return pl.pallas_call(
            functools.partial(first_kernel, "tensor", count, pieces),
            out_shape=jax.ShapeDtypeStruct((2, pieces, rows + 16, cols), jnp.int16),
            in_specs=[vmem, hbm],
            out_specs=hbm,
            scratch_shapes=[
                pltpu.VMEM((pieces, depth, cols), jnp.bfloat16),
                packed(pieces),
                dma((pieces,)),
                dma((pieces,)),
                dma((2, pieces)),
            ],
            compiler_params=params(0),
            cost_estimate=cost(45),
        )(hidden, weight)

    def rest(got):
        return pl.pallas_call(
            functools.partial(rest_kernel, "tensor", count, pieces),
            out_shape=jax.ShapeDtypeStruct((pieces, rows, cols), jnp.float32),
            in_specs=[vmem, hbm, hbm],
            out_specs=vmem,
            scratch_shapes=[
                pltpu.VMEM((total, depth, cols), jnp.bfloat16),
                packed(2 * pieces),
                packed(total + pieces),
                dma((total,)),
                dma((2, pieces)),
                dma((2, total)),
                dma((2, total)),
            ],
            compiler_params=params(1),
            cost_estimate=cost(90),
        )(hidden, weight, got)

    return first, rest


def sum_kernel(axis, count, in_ref, out_ref, parts, full, send_sem, recv_sem):
    me = lax.axis_index(axis)
    size = parts.shape[1]

    def peer(k):
        return lax.rem(me + k, count)

    barrier = pltpu.get_barrier_semaphore()
    for k in range(1, count):
        pl.semaphore_signal(barrier, inc=1, device_id={axis: peer(k)}, device_id_type=MESH)
    pl.semaphore_wait(barrier, count - 1)

    def scatter(k):
        return pltpu.make_async_remote_copy(
            src_ref=in_ref.at[pl.ds(peer(k) * size, size)],
            dst_ref=parts.at[k],
            send_sem=send_sem.at[0, k],
            recv_sem=recv_sem.at[0, k],
            device_id={axis: peer(k)},
            device_id_type=MESH,
        )

    def gather(k):
        mine = full.at[pl.ds(me * size, size)]
        return pltpu.make_async_remote_copy(
            src_ref=mine,
            dst_ref=mine,
            send_sem=send_sem.at[1, k],
            recv_sem=recv_sem.at[1, k],
            device_id={axis: peer(k)},
            device_id_type=MESH,
        )

    for k in range(1, count):
        scatter(k).start()
    total = in_ref[pl.ds(me * size, size)]
    for k in range(1, count):
        scatter(k).wait_recv()
        total = total + parts[k]
    full[pl.ds(me * size, size)] = total
    for k in range(1, count):
        gather(k).start()
    for k in range(1, count):
        gather(k).wait_recv()
    out_ref[...] = full[...]
    for k in range(1, count):
        scatter(k).wait_send()
        gather(k).wait_send()


def sum_over_tensor(x):
    count = lax.axis_size("tensor")
    size = x.shape[0] // count
    vmem = pl.BlockSpec(memory_space=pltpu.VMEM)
    return pl.pallas_call(
        functools.partial(sum_kernel, "tensor", count),
        out_shape=jax.ShapeDtypeStruct(x.shape, x.dtype),
        in_specs=[vmem],
        out_specs=vmem,
        scratch_shapes=[
            pltpu.VMEM((count, size) + x.shape[1:], x.dtype),
            pltpu.VMEM(x.shape, x.dtype),
            pltpu.SemaphoreType.DMA((2, count)),
            pltpu.SemaphoreType.DMA((2, count)),
        ],
        compiler_params=pltpu.CompilerParams(
            collective_id=2, has_side_effects=True, vmem_limit_bytes=16 * MIB
        ),
    )(x)


def join_kernel(held_ref, rel_ref, base_ref, *refs):
    deltas, out_ref = refs[:-1], refs[-1]
    pieces, _, cols = base_ref.shape
    block = deltas[0].shape[1]
    for i in range(PAIR):
        span = slice(i * block, (i + 1) * block)
        for k, delta in enumerate(deltas[i::PAIR]):
            @pl.when(rel_ref[pl.program_id(0) * PAIR + i] == k)
            def _():
                for c in range(pieces):
                    part = slice(c * cols, (c + 1) * cols)
                    out_ref[span, part] = (base_ref[c, span] + delta[0, :, part]).astype(
                        out_ref.dtype
                    )


def join(base, deltas, held, rel):
    pieces, rows, cols = base.shape
    segs = rel.shape[0]
    _, block, width = deltas[0].shape

    def spec(k, i):
        return pl.BlockSpec(
            (1, block, width), lambda s, held, rel: (held[k * segs + s * PAIR + i], 0, 0)
        )

    return pl.pallas_call(
        join_kernel,
        grid_spec=pltpu.PrefetchScalarGridSpec(
            num_scalar_prefetch=2,
            grid=(segs // PAIR,),
            in_specs=[pl.BlockSpec((pieces, PAIR * block, cols), lambda s, held, rel: (0, s, 0))]
            + [spec(k, i) for k in range(len(deltas)) for i in range(PAIR)],
            out_specs=pl.BlockSpec((PAIR * block, width), lambda s, held, rel: (s, 0)),
        ),
        out_shape=jax.ShapeDtypeStruct((rows, width), jnp.bfloat16),
        compiler_params=pltpu.CompilerParams(vmem_limit_bytes=16 * MIB),
    )(held, rel, base, *[d for d in deltas for _ in range(PAIR)])


def shift(x, by, count):
    return lax.ppermute(x, "dp", [(i, (i + by) % count) for i in range(count)])


def per_device(
    hidden, output_weight, adapter_down_maps, adapter_up_maps, adapter_slot, segment_adapter
):
    rows, width = hidden.shape
    segs = segment_adapter.shape[0]
    block = rows // segs
    stored, rank_dim, _ = adapter_down_maps.shape
    dp = lax.axis_size("dp")
    me = lax.axis_index("dp")
    cap = segs // 2
    slot = adapter_slot[segment_adapter]
    rel = (slot // stored - me) % dp
    local = slot % stored
    mask = rel[None, :] == jnp.arange(dp, dtype=jnp.int32)[:, None]
    running = jnp.cumsum(mask.astype(jnp.int32), axis=1) - 1
    position = jnp.sum(jnp.where(mask, running, 0), axis=0)
    match = mask[:, None, :] & (
        position[None, None, :] == jnp.arange(cap, dtype=jnp.int32)[None, :, None]
    )
    picked = jnp.sum(
        jnp.where(match, jnp.arange(segs, dtype=jnp.int32)[None, None, :], 0), axis=2
    )
    wanted = jnp.sum(jnp.where(match, local[None, None, :], 0), axis=2)
    held = jnp.clip(running, 0, cap - 1).astype(jnp.int32).reshape(-1)
    seg_rows = hidden.reshape(segs, block, width)
    got_slots = [wanted[0]] + [shift(wanted[k], k, dp) for k in range(1, dp)]
    got_rows = [seg_rows[picked[0]]] + [
        shift(seg_rows[picked[k]], k, dp) for k in range(1, dp)
    ]
    slots = jnp.concatenate(got_slots)
    there_rows = jnp.concatenate(got_rows)
    first, rest = base_parts(hidden, output_weight)
    part, there_rows = lax.optimization_barrier((first(), there_rows))
    rank = apply_maps(down_kernel, slots, there_rows, adapter_down_maps, (block, 2 * rank_dim), 1, 2)
    rank = sum_over_tensor(rank)
    delta = apply_maps(up_kernel, slots, rank, adapter_up_maps, (block, width), 2, 1)
    part, delta = lax.optimization_barrier((part, delta))
    delta = delta.reshape(dp, cap, block, width)
    back = [delta[0]] + [shift(delta[k], dp - k, dp) for k in range(1, dp)]
    return join(rest(part), back, held, rel.astype(jnp.int32))


def solution(mesh):
    return jax.shard_map(
        per_device,
        mesh=mesh,
        in_specs=(
            P(("groups", "dp"), "tensor"),
            P("tensor", None),
            P("dp", None, "tensor"),
            P("dp", None, "tensor"),
            P("groups"),
            P(("groups", "dp")),
        ),
        out_specs=P(("groups", "dp"), "tensor"),
        check_vma=False,
    )
```
